32 devices in a mesh: dp: 4 (over x, core), sp: 8 (over z, y).
Axes of the slice: x: 2, y: 2, z: 4, core: 2. Of those that a mesh axis runs over, the one named last changes fastest.
Arguments:
- frames_in: bfloat16 [2048, 64, 256], P(('dp', 'sp')), may hold values from -6 to 6
- spatial_weight: bfloat16 [3, 3, 256, 256], replicated, may hold values from -0.125 to 0.125
- temporal_weight: bfloat16 [3, 256, 256], replicated, may hold values from -0.21875 to 0.21875
- cotangent: bfloat16 [2048, 64, 256], P(('dp', 'sp')), may hold values from -6 to 6
Outputs:
- block_out: bfloat16 [2048, 64, 256], P(('dp', 'sp'))
- grad_input: bfloat16 [2048, 64, 256], P(('dp', 'sp'))
- grad_spatial: float32 [3, 3, 256, 256], replicated
- grad_temporal: float32 [3, 256, 256], replicated
The draws below stay inside these ranges and needn't reach their ends.
All inputs are finite; a program needn't handle non-finite values.
Results may differ from the reference program's by a relative error of at most 0.0049.
Values may be sent and summed in bfloat16 or wider, within the bound.
A program may use at most 128 MiB of HBM per device.

```python
import math
import jax
import jax.numpy as jnp

C = 256
H = 64
W = 64
FRAMES = 4
ROWS = 2048


def levels(stream_key, dims, split, low, top_value):
    factor_of, own = 1.0, jax.random.fold_in(stream_key, 6)
    for dim, blocks in split:
        draws = jnp.exp(jax.random.uniform(jax.random.fold_in(own, dim), (blocks,), jnp.float32, low / len(split), top_value / len(split)))
        factor_of = factor_of * jnp.repeat(draws, dims[dim] // blocks).reshape([-1 if axis == dim else 1 for axis in range(len(dims))])
    return factor_of


def noise(rng, shape, scale, most, pieces=(), kind=jnp.bfloat16):
    values = jax.random.normal(rng, shape, jnp.float32) * scale
    if len(pieces) > 0:
        values = levels(rng, shape, pieces, -0.22, 0.18) * values
    return jnp.clip(values, min=-most, max=most).astype(kind)


def setup_inputs(seed: int = 0) -> dict:
    seeds = jax.random.split(jax.random.key(seed), 5)
    frames_in = noise(seeds[0], (ROWS, W, C), 1.0, 6.0, ((0, 32),))
    spatial_weight = noise(seeds[1], (3, 3, C, C), (9 * C) ** -0.5, 0.125)
    temporal_weight = noise(seeds[2], (3, C, C), (3 * C) ** -0.5, 0.21875)
    cotangent = noise(seeds[3], (ROWS, W, C), 1.0, 6.0, ((0, 32),))
    return {"frames_in": frames_in, "spatial_weight": spatial_weight, "temporal_weight": temporal_weight, "cotangent": cotangent}


def reference(frames_in, spatial_weight, temporal_weight, cotangent):
    total_rows, width_cells, channels = frames_in.shape
    frame_count = total_rows // H
    clip_count = frame_count // FRAMES
    frames_grid = frames_in.reshape(frame_count, H, width_cells, channels)
    padded_in = jnp.pad(frames_grid, ((0, 0), (1, 1), (1, 1), (0, 0)))
    pre = jnp.zeros((frame_count * H * width_cells, channels), jnp.float32)
    for tap_row in range(3):
        for tap_col in range(3):
            window = padded_in[:, tap_row:tap_row + H, tap_col:tap_col + width_cells].reshape(-1, channels)
            pre = pre + jnp.dot(window, spatial_weight[tap_row, tap_col], preferred_element_type=jnp.float32)
    act = jax.nn.silu(pre).astype(jnp.bfloat16)
    act_clips = act.reshape(clip_count, FRAMES, H * width_cells, channels)
    act_padded = jnp.pad(act_clips, ((0, 0), (2, 0), (0, 0), (0, 0)))
    cot_clips = cotangent.reshape(clip_count, FRAMES, H * width_cells, channels)
    cot_padded = jnp.pad(cot_clips, ((0, 0), (0, 2), (0, 0), (0, 0)))
    cot_flat = cotangent.reshape(-1, channels)
    temporal_out = jnp.zeros((total_rows * width_cells, channels), jnp.float32)
    grad_act = jnp.zeros((total_rows * width_cells, channels), jnp.float32)
    temporal_terms = []
    for tap_step in range(3):
        earlier = act_padded[:, 2 - tap_step:2 - tap_step + FRAMES].reshape(-1, channels)
        temporal_out = temporal_out + jnp.dot(earlier, temporal_weight[tap_step], preferred_element_type=jnp.float32)
        temporal_terms.append(jnp.dot(earlier.T, cot_flat, preferred_element_type=jnp.float32))
        later = cot_padded[:, tap_step:tap_step + FRAMES].reshape(-1, channels)
        grad_act = grad_act + jnp.dot(later, temporal_weight[tap_step].T, preferred_element_type=jnp.float32)
    temporal_out = temporal_out.astype(jnp.bfloat16)
    block_out = (frames_in.reshape(-1, channels).astype(jnp.float32) + temporal_out.astype(jnp.float32)).astype(jnp.bfloat16)
    grad_act = grad_act.astype(jnp.bfloat16)
    sigma = jax.nn.sigmoid(pre)
    grad_pre = (grad_act.astype(jnp.float32) * (sigma * (1.0 + pre * (1.0 - sigma)))).astype(jnp.bfloat16)
    grad_flat = grad_pre.reshape(-1, channels)
    grad_grid = grad_pre.reshape(frame_count, H, width_cells, channels)
    grad_padded = jnp.pad(grad_grid, ((0, 0), (1, 1), (1, 1), (0, 0)))
    spatial_terms = []
    grad_in = cot_flat.astype(jnp.float32)
    for tap_row in range(3):
        for tap_col in range(3):
            window = padded_in[:, tap_row:tap_row + H, tap_col:tap_col + width_cells].reshape(-1, channels)
            spatial_terms.append(jnp.dot(window.T, grad_flat, preferred_element_type=jnp.float32))
            back_window = grad_padded[:, 2 - tap_row:2 - tap_row + H, 2 - tap_col:2 - tap_col + width_cells].reshape(-1, channels)
            grad_in = grad_in + jnp.dot(back_window, spatial_weight[tap_row, tap_col].T, preferred_element_type=jnp.float32)
    grad_scale = 1.0 / math.sqrt(total_rows * width_cells)
    grad_spatial = jnp.stack(spatial_terms).reshape(3, 3, channels, channels) * grad_scale
    grad_temporal = jnp.stack(temporal_terms) * grad_scale
    shape_out = (total_rows, width_cells, channels)
    return (block_out.reshape(shape_out), grad_in.astype(jnp.bfloat16).reshape(shape_out), grad_spatial, grad_temporal)
```

```python
import functools
import math

import jax
import jax.numpy as jnp
from jax import lax
from jax.experimental import pallas as pl
from jax.experimental.pallas import tpu as pltpu
from jax.sharding import PartitionSpec as P

FRAMES = 4
BLOCKS = 4
VMEM_LIMIT = 50 * 1024 * 1024
MESH = pl.DeviceIdType.MESH
F32 = jnp.float32
BF16 = jnp.bfloat16


def store_shifted(dest, offset, values, width):
    cells, channels = values.shape
    column = lax.broadcasted_iota(jnp.int32, (cells, channels), 0) % width
    before = jnp.where(column == 0, 0.0, pltpu.roll(values, 1, axis=0))
    after = jnp.where(column == width - 1, 0.0, pltpu.roll(values, cells - 1, axis=0))
    dest[pl.ds(offset, cells), 0:channels] = before.astype(BF16)
    dest[pl.ds(offset, cells), channels : 2 * channels] = values.astype(BF16)
    dest[pl.ds(offset, cells), 2 * channels : 3 * channels] = after.astype(BF16)


def zero_edges(dest, width):
    rows, lanes = dest.shape
    dest[0:width] = jnp.zeros((width, lanes), BF16)
    dest[rows - width : rows] = jnp.zeros((width, lanes), BF16)


def forward_kernel(width, x_ref, w_ref, act_ref, slope_ref, x3):
    step = pl.program_id(0)
    cells, channels = act_ref.shape

    @pl.when(step == 0)
    def _():
        zero_edges(x3, width)
        for block in range(BLOCKS):
            store_shifted(
                x3,
                width + block * cells,
                x_ref[block * cells : (block + 1) * cells].astype(F32),
                width,
            )

    base = pl.multiple_of(step * cells, cells)
    pre = jnp.zeros((cells, channels), F32)
    for tap in range(3):
        pre = pre + jnp.dot(
            x3[pl.ds(base + tap * width, cells), :], w_ref[tap], preferred_element_type=F32
        )
    sigma = jax.nn.sigmoid(pre)
    act_ref[...] = (pre * sigma).astype(BF16)
    slope_ref[...] = (sigma * (1.0 + pre * (1.0 - sigma))).astype(BF16)


def backward_kernel(
    width, x_ref, cot_ref, cot1_ref, cot2_ref, act_ref, slope_ref, wt_ref, wf_ref,
    grad_in_ref, grads_ref, g3, temporal, spatial,
):
    step = pl.program_id(0)
    cells, channels = act_ref.shape

    @pl.when(step == 0)
    def _():
        zero_edges(g3, width)
        temporal[...] = jnp.zeros_like(temporal)
        spatial[...] = jnp.zeros_like(spatial)

    @pl.when(step < BLOCKS)
    def _():
        act_t = act_ref[...].T
        grad_act = jnp.zeros((cells, channels), F32)
        for tap, ref in enumerate((cot_ref, cot1_ref, cot2_ref)):
            grad_act = grad_act + jnp.dot(ref[...], wt_ref[tap], preferred_element_type=F32)
            temporal[tap] += jnp.dot(act_t, ref[...], preferred_element_type=F32)
        grad_pre = grad_act * slope_ref[...].astype(F32)
        store_shifted(g3, pl.multiple_of(width + step * cells, width), grad_pre, width)

    @pl.when(step >= BLOCKS)
    def _():
        base = pl.multiple_of((step - BLOCKS) * cells, cells)
        x_t = x_ref[...].T
        grad_in = cot_ref[...].astype(F32)
        for tap in range(3):
            window = g3[pl.ds(base + tap * width, cells), :]
            grad_in = grad_in + jnp.dot(window, wf_ref[tap], preferred_element_type=F32)
            spatial[tap] += jnp.dot(x_t, window, preferred_element_type=F32)
        grad_in_ref[...] = grad_in.astype(BF16)

    @pl.when(step == 2 * BLOCKS - 1)
    def _():
        for tap_row in range(3):
            for tap_col in range(3):
                place = (2 - tap_row) * 3 + 2 - tap_col
                grads_ref[place * channels : (place + 1) * channels] = spatial[
                    tap_row, :, tap_col * channels : (tap_col + 1) * channels
                ]
        for tap in range(3):
            grads_ref[(9 + tap) * channels : (10 + tap) * channels] = temporal[tap]


def temporal_kernel(x_ref, act_ref, act1_ref, act2_ref, w_ref, out_ref):
    total = jnp.dot(act_ref[...], w_ref[0], preferred_element_type=F32)
    total = total + jnp.dot(act1_ref[...], w_ref[1], preferred_element_type=F32)
    total = total + jnp.dot(act2_ref[...], w_ref[2], preferred_element_type=F32)
    total = total.astype(BF16).astype(F32)
    out_ref[...] = (x_ref[...].astype(F32) + total).astype(BF16)


def reduce_kernel(bits, grads_ref, full_ref, total, *scratch):
    levels = len(bits)
    sends, recvs = scratch[:levels], scratch[levels : 2 * levels]
    send_sem, recv_sem, back_send, back_recv = scratch[2 * levels :]
    here = {name: lax.axis_index(name) for name in ("dp", "sp")}

    def partner(level):
        name, bit = bits[level]
        mine = (here[name] // (1 << bit)) % 2
        other = here[name] + (1 - 2 * mine) * (1 << bit)
        ids = dict(here)
        ids[name] = other
        return mine, (ids["dp"], ids["sp"])

    partners = [partner(level) for level in range(levels)]
    barrier = pltpu.get_barrier_semaphore()
    for _, device in partners:
        pl.semaphore_signal(barrier, inc=1, device_id=device, device_id_type=MESH)
    pl.semaphore_wait(barrier, levels)

    rows = grads_ref.shape[0]
    half = grads_ref.shape[1] // 2

    def exchange(level):
        copy = pltpu.make_async_remote_copy(
            src_ref=sends[level],
            dst_ref=recvs[level],
            send_sem=send_sem.at[level],
            recv_sem=recv_sem.at[level],
            device_id=partners[level][1],
            device_id_type=MESH,
        )
        copy.start()
        return copy

    mine, _ = partners[0]
    keep = pl.multiple_of(mine * half, half)
    give = pl.multiple_of((1 - mine) * half, half)
    sends[0][...] = grads_ref[:, pl.ds(give, half)].astype(BF16)
    copy = exchange(0)
    copy.wait()
    total[...] = grads_ref[:, pl.ds(keep, half)] + recvs[0][...].astype(F32)
    start = 0
    size = rows
    starts = []
    for level in range(1, levels):
        size = size // 2
        mine, _ = partners[level]
        own = pl.multiple_of(start + mine * size, 16)
        other = pl.multiple_of(start + (1 - mine) * size, 16)
        sends[level][...] = total[pl.ds(other, size), :].astype(BF16)
        copy = exchange(level)
        copy.wait()
        total[pl.ds(own, size), :] += recvs[level][...].astype(F32)
        start = own
        starts.append(own)
    full_ref[pl.ds(start, size), pl.ds(keep, half)] = total[pl.ds(start, size), :].astype(BF16)
    for level in range(levels - 1, -1, -1):
        if level:
            own = pl.multiple_of(starts[level - 1], 16)
            place = full_ref.at[pl.ds(own, size), pl.ds(keep, half)]
        else:
            place = full_ref.at[:, pl.ds(keep, half)]
        copy = pltpu.make_async_remote_copy(
            src_ref=place,
            dst_ref=place,
            send_sem=back_send.at[level],
            recv_sem=back_recv.at[level],
            device_id=partners[level][1],
            device_id_type=MESH,
        )
        copy.start()
        copy.wait()
        size = size * 2


def reduce_all(grads):
    bits = []
    for name in ("dp", "sp"):
        count = lax.axis_size(name)
        bits += [(name, bit) for bit in range(count.bit_length() - 1)]
    rows, channels = grads.shape
    sizes = [rows >> level for level in range(len(bits))]
    pieces = [pltpu.VMEM((size, channels // 2), BF16) for size in sizes]
    semaphores = [pltpu.SemaphoreType.DMA((len(bits),))] * 4
    return pl.pallas_call(
        functools.partial(reduce_kernel, bits),
        out_shape=jax.ShapeDtypeStruct((rows, channels), BF16),
        in_specs=[pl.BlockSpec(memory_space=pltpu.VMEM)],
        out_specs=pl.BlockSpec(memory_space=pltpu.VMEM),
        scratch_shapes=[pltpu.VMEM((rows, channels // 2), F32)] + pieces + pieces + semaphores,
        compiler_params=pltpu.CompilerParams(
            collective_id=0, has_side_effects=True, vmem_limit_bytes=VMEM_LIMIT
        ),
        name="reduce_all",
    )(grads)


def whole(array):
    return pl.BlockSpec(array.shape, lambda step: (0,) * array.ndim)


def local(frames_in, spatial_weight, temporal_weight, cotangent):
    slab_rows, width, channels = frames_in.shape
    sp_count = lax.axis_size("sp")
    cells = slab_rows * width
    block = cells // BLOCKS
    x = frames_in.reshape(cells, channels)
    cot = cotangent.reshape(cells, channels)
    params = pltpu.CompilerParams(
        dimension_semantics=("arbitrary",), vmem_limit_bytes=VMEM_LIMIT
    )

    def shift(values, by):
        pairs = [
            (i, i + by)
            for i in range(sp_count)
            if 0 <= i + by < sp_count and (i + by) // FRAMES == i // FRAMES
        ]
        return lax.ppermute(values, "sp", pairs)

    cot1 = shift(cot, -1)
    cot2 = shift(cot, -2)

    w3 = spatial_weight.reshape(3, 3 * channels, channels)
    wf = spatial_weight[::-1, ::-1].transpose(0, 1, 3, 2).reshape(3, 3 * channels, channels)
    wt = temporal_weight.transpose(0, 2, 1)
    rows_spec = pl.BlockSpec((block, channels), lambda step: (step, 0))
    frame = jax.ShapeDtypeStruct((cells, channels), BF16)
    padded = pltpu.VMEM((cells + 2 * width, 3 * channels), BF16)

    act, slope = pl.pallas_call(
        functools.partial(forward_kernel, width),
        grid=(BLOCKS,),
        out_shape=(frame, frame),
        in_specs=[whole(x), whole(w3)],
        out_specs=(rows_spec, rows_spec),
        scratch_shapes=[padded],
        compiler_params=params,
        cost_estimate=pl.CostEstimate(
            flops=18 * cells * channels * channels,
            bytes_accessed=8 * cells * channels,
            transcendentals=2 * cells * channels,
        ),
        name="forward",
    )(x, w3)

    act1 = shift(act, 1)
    act2 = shift(act, 2)

    first = pl.BlockSpec((block, channels), lambda step: (jnp.minimum(step, BLOCKS - 1), 0))
    second = pl.BlockSpec((block, channels), lambda step: (jnp.maximum(step - BLOCKS, 0), 0))
    both = pl.BlockSpec((block, channels), lambda step: (step % BLOCKS, 0))
    grads_shape = jax.ShapeDtypeStruct((12 * channels, channels), F32)
    grad_in, grads = pl.pallas_call(
        functools.partial(backward_kernel, width),
        grid=(2 * BLOCKS,),
        out_shape=(frame, grads_shape),
        in_specs=[second, both, first, first, first, first, whole(wt), whole(wf)],
        out_specs=(second, whole(grads_shape)),
        scratch_shapes=[
            padded,
            pltpu.VMEM((3, channels, channels), F32),
            pltpu.VMEM((3, channels, 3 * channels), F32),
        ],
        compiler_params=params,
        cost_estimate=pl.CostEstimate(
            flops=48 * cells * channels * channels,
            bytes_accessed=18 * cells * channels,
            transcendentals=0,
        ),
        name="backward",
    )(x, cot, cot1, cot2, act, slope, wt, wf)

    reduced = reduce_all(grads)

    block_out = pl.pallas_call(
        temporal_kernel,
        grid=(BLOCKS,),
        out_shape=frame,
        in_specs=[rows_spec] * 4 + [whole(temporal_weight)],
        out_specs=rows_spec,
        compiler_params=params,
        cost_estimate=pl.CostEstimate(
            flops=6 * cells * channels * channels,
            bytes_accessed=10 * cells * channels,
            transcendentals=0,
        ),
        name="temporal",
    )(x, act, act1, act2, temporal_weight)

    grad_scale = 1.0 / math.sqrt(slab_rows * sp_count * lax.axis_size("dp") * width)
    scaled = reduced.astype(F32) * grad_scale
    grad_spatial = scaled[: 9 * channels].reshape(3, 3, channels, channels)
    grad_temporal = scaled[9 * channels :].reshape(3, channels, channels)
    return (
        block_out.reshape(frames_in.shape),
        grad_in.reshape(frames_in.shape),
        grad_spatial,
        grad_temporal,
    )


def solution(mesh):
    placed = (P(("dp", "sp"), None, None), P(), P(), P(("dp", "sp"), None, None))
    return jax.shard_map(
        local,
        mesh=mesh,
        in_specs=placed,
        out_specs=(P(("dp", "sp"), None, None), P(("dp", "sp"), None, None), P(), P()),
        check_vma=False,
    )
```

```python
import functools
import math

import jax
import jax.numpy as jnp
from jax import lax
from jax.experimental import pallas as pl
from jax.experimental.pallas import tpu as pltpu
from jax.sharding import PartitionSpec as P

FRAMES = 4
BLOCKS = 4
VMEM_LIMIT = 50 * 1024 * 1024
MESH = pl.DeviceIdType.MESH
F32 = jnp.float32
BF16 = jnp.bfloat16


def store_shifted(dest, offset, values, width):
    cells, channels = values.shape
    column = lax.broadcasted_iota(jnp.int32, (cells, channels), 0) % width
    before = jnp.where(column == 0, 0.0, pltpu.roll(values, 1, axis=0))
    after = jnp.where(column == width - 1, 0.0, pltpu.roll(values, cells - 1, axis=0))
    dest[pl.ds(offset, cells), 0:channels] = before.astype(BF16)
    dest[pl.ds(offset, cells), channels : 2 * channels] = values.astype(BF16)
    dest[pl.ds(offset, cells), 2 * channels : 3 * channels] = after.astype(BF16)


def zero_edges(dest, width):
    rows, lanes = dest.shape
    dest[0:width] = jnp.zeros((width, lanes), BF16)
    dest[rows - width : rows] = jnp.zeros((width, lanes), BF16)


def forward_kernel(width, x_ref, w_ref, act_ref, slope_ref, x3):
    step = pl.program_id(0)
    cells, channels = act_ref.shape

    @pl.when(step == 0)
    def _():
        zero_edges(x3, width)
        for block in range(BLOCKS):
            store_shifted(
                x3,
                width + block * cells,
                x_ref[block * cells : (block + 1) * cells].astype(F32),
                width,
            )

    base = pl.multiple_of(step * cells, cells)
    pre = jnp.zeros((cells, channels), F32)
    for tap in range(3):
        pre = pre + jnp.dot(
            x3[pl.ds(base + tap * width, cells), :], w_ref[tap], preferred_element_type=F32
        )
    sigma = jax.nn.sigmoid(pre)
    act_ref[...] = (pre * sigma).astype(BF16)
    slope_ref[...] = sigma * (1.0 + pre * (1.0 - sigma))


def backward_kernel(
    width, x_ref, cot_ref, near_ref, far_lo_ref, far_hi_ref, via_lo_ref, via_hi_ref, act_ref, slope_ref, wt_ref, wf_ref,
    grad_in_ref, grads_ref, g3, temporal, spatial,
):
    step = pl.program_id(0)
    cells, channels = act_ref.shape

    @pl.when(step == 0)
    def _():
        zero_edges(g3, width)
        temporal[...] = jnp.zeros_like(temporal)
        spatial[...] = jnp.zeros_like(spatial)

    @pl.when(step < BLOCKS)
    def _():
        act_t = act_ref[...].T
        grad_act = jnp.zeros((cells, channels), F32)
        low = step < BLOCKS // 2
        next1 = near_ref[...] + jnp.where(low, via_lo_ref[...], via_hi_ref[...])
        next2 = jnp.where(low, far_lo_ref[...], far_hi_ref[...])
        for tap, later in enumerate((cot_ref[...], next1, next2)):
            grad_act = grad_act + jnp.dot(later, wt_ref[tap], preferred_element_type=F32)
            temporal[tap] += jnp.dot(act_t, later, preferred_element_type=F32)
        grad_pre = grad_act * slope_ref[...]
        store_shifted(g3, pl.multiple_of(width + step * cells, width), grad_pre, width)

    @pl.when(step >= BLOCKS)
    def _():
        base = pl.multiple_of((step - BLOCKS) * cells, cells)
        x_t = x_ref[...].T
        grad_in = cot_ref[...].astype(F32)
        for tap in range(3):
            window = g3[pl.ds(base + tap * width, cells), :]
            grad_in = grad_in + jnp.dot(window, wf_ref[tap], preferred_element_type=F32)
            spatial[tap] += jnp.dot(x_t, window, preferred_element_type=F32)
        grad_in_ref[...] = grad_in.astype(BF16)

    @pl.when(step == 2 * BLOCKS - 1)
    def _():
        for tap_row in range(3):
            for tap_col in range(3):
                place = (2 - tap_row) * 3 + 2 - tap_col
                grads_ref[place * channels : (place + 1) * channels] = spatial[
                    tap_row, :, tap_col * channels : (tap_col + 1) * channels
                ]
        for tap in range(3):
            grads_ref[(9 + tap) * channels : (10 + tap) * channels] = temporal[tap]


def temporal_kernel(x_ref, act_ref, act1_ref, act2_ref, w_ref, out_ref):
    total = jnp.dot(act_ref[...], w_ref[0], preferred_element_type=F32)
    total = total + jnp.dot(act1_ref[...], w_ref[1], preferred_element_type=F32)
    total = total + jnp.dot(act2_ref[...], w_ref[2], preferred_element_type=F32)
    total = total.astype(BF16).astype(F32)
    out_ref[...] = (x_ref[...].astype(F32) + total).astype(BF16)


def reduce_kernel(bits, chunks, grads_ref, full_ref, total, *scratch):
    levels = len(bits)
    staged = scratch[:chunks]
    recvs = scratch[chunks : chunks + chunks * levels]
    send_sem, recv_sem, back_send, back_recv = scratch[chunks + chunks * levels :]
    here = {name: lax.axis_index(name) for name in ("dp", "sp")}

    def partner(name, bit):
        mine = (here[name] // (1 << bit)) % 2
        ids = dict(here)
        ids[name] = here[name] + (1 - 2 * mine) * (1 << bit)
        return mine, (ids["dp"], ids["sp"])

    partners = [partner(name, bit) for name, bit in bits]
    barrier = pltpu.get_barrier_semaphore()
    for _, device in partners:
        pl.semaphore_signal(barrier, inc=1, device_id=device, device_id_type=MESH)
    pl.semaphore_wait(barrier, levels)

    rows = grads_ref.shape[0] // chunks
    half = grads_ref.shape[1] // 2
    rest = partners[1:]
    orders = []
    for chunk in range(chunks):
        turn = chunk % len(rest)
        orders.append(partners[:1] + rest[turn:] + rest[:turn])

    def send(chunk, level, source, dest, send_sems, recv_sems):
        copy = pltpu.make_async_remote_copy(
            src_ref=source,
            dst_ref=dest,
            send_sem=send_sems.at[chunk * levels + level],
            recv_sem=recv_sems.at[chunk * levels + level],
            device_id=orders[chunk][level][1],
            device_id_type=MESH,
        )
        copy.start()
        return copy

    mine = partners[0][0]
    keep = pl.multiple_of(mine * half, half)
    give = pl.multiple_of((1 - mine) * half, half)
    copies = [
        send(
            chunk, 0, grads_ref.at[chunk * rows : (chunk + 1) * rows, pl.ds(give, half)],
            recvs[chunk * levels], send_sem, recv_sem,
        )
        for chunk in range(chunks)
    ]
    for chunk in range(chunks):
        copies[chunk].wait()
        place = pl.ds(chunk * rows, rows)
        total[place, :] = grads_ref[place, pl.ds(keep, half)] + recvs[chunk * levels][...]
    starts = [[chunk * rows] for chunk in range(chunks)]
    size = rows
    for level in range(1, levels):
        size = size // 2
        copies = []
        for chunk in range(chunks):
            mine = orders[chunk][level][0]
            start = starts[chunk][-1]
            own = pl.multiple_of(start + mine * size, 16)
            other = pl.multiple_of(start + (1 - mine) * size, 16)
            source = total.at[pl.ds(other, size), :]
            if level == 1:
                staged[chunk][...] = total[pl.ds(other, size), :].astype(BF16)
                source = staged[chunk]
            dest = recvs[chunk * levels + level]
            copies.append(send(chunk, level, source, dest, send_sem, recv_sem))
            starts[chunk].append(own)
        for chunk in range(chunks):
            copies[chunk].wait()
            arrived = recvs[chunk * levels + level][...].astype(F32)
            total[pl.ds(starts[chunk][-1], size), :] += arrived
    for chunk in range(chunks):
        place = pl.ds(starts[chunk][-1], size)
        full_ref[place, pl.ds(keep, half)] = total[place, :].astype(BF16)
    for level in range(levels - 1, -1, -1):
        copies = []
        for chunk in range(chunks):
            place = full_ref.at[pl.ds(starts[chunk][level], size), pl.ds(keep, half)]
            copies.append(send(chunk, level, place, place, back_send, back_recv))
        for copy in copies:
            copy.wait()
        size = size * 2


def reduce_all(grads):
    bits = []
    for name in ("dp", "sp"):
        count = lax.axis_size(name)
        bits += [(name, bit) for bit in range(count.bit_length() - 1)]
    total_rows, channels = grads.shape
    half = channels // 2
    chunks = 3
    rows = total_rows // chunks
    levels = len(bits)
    staged = [pltpu.VMEM((rows // 2, half), BF16)] * chunks
    recvs = [
        pltpu.VMEM((rows >> level, half), BF16 if level == 1 else F32)
        for _ in range(chunks)
        for level in range(levels)
    ]
    semaphores = [pltpu.SemaphoreType.DMA((chunks * levels,))] * 4
    return pl.pallas_call(
        functools.partial(reduce_kernel, bits, chunks),
        out_shape=jax.ShapeDtypeStruct(grads.shape, BF16),
        in_specs=[pl.BlockSpec(memory_space=pltpu.VMEM)],
        out_specs=pl.BlockSpec(memory_space=pltpu.VMEM),
        scratch_shapes=[pltpu.VMEM((total_rows, half), F32)] + staged + recvs + semaphores,
        compiler_params=pltpu.CompilerParams(
            collective_id=0, has_side_effects=True, vmem_limit_bytes=VMEM_LIMIT
        ),
        name="reduce_all",
    )(grads)


def whole(array):
    return pl.BlockSpec(array.shape, lambda step: (0,) * array.ndim)


def local(frames_in, spatial_weight, temporal_weight, cotangent):
    slab_rows, width, channels = frames_in.shape
    sp_count = lax.axis_size("sp")
    cells = slab_rows * width
    block = cells // BLOCKS
    x = frames_in.reshape(cells, channels)
    cot = cotangent.reshape(cells, channels)
    params = pltpu.CompilerParams(
        dimension_semantics=("arbitrary",), vmem_limit_bytes=VMEM_LIMIT
    )

    def move(values, *steps):
        pairs = [
            (clip + source, clip + target)
            for clip in range(0, sp_count, FRAMES)
            for source, target in steps
        ]
        return lax.ppermute(values, "sp", pairs)

    middle = cells // 2
    far_lo = move(cot[:middle], (2, 0), (3, 1))
    near = move(cot, (1, 0), (3, 2))
    far_hi = move(cot[middle:], (2, 0), (3, 1))

    w3 = spatial_weight.reshape(3, 3 * channels, channels)
    wf = spatial_weight[::-1, ::-1].transpose(0, 1, 3, 2).reshape(3, 3 * channels, channels)
    wt = temporal_weight.transpose(0, 2, 1)
    rows_spec = pl.BlockSpec((block, channels), lambda step: (step, 0))
    frame = jax.ShapeDtypeStruct((cells, channels), BF16)
    padded = pltpu.VMEM((cells + 2 * width, 3 * channels), BF16)

    act, slope = pl.pallas_call(
        functools.partial(forward_kernel, width),
        grid=(BLOCKS,),
        out_shape=(frame, jax.ShapeDtypeStruct((cells, channels), F32)),
        in_specs=[whole(x), whole(w3)],
        out_specs=(rows_spec, rows_spec),
        scratch_shapes=[padded],
        compiler_params=params,
        cost_estimate=pl.CostEstimate(
            flops=18 * cells * channels * channels,
            bytes_accessed=8 * cells * channels,
            transcendentals=2 * cells * channels,
        ),
        name="forward",
    )(x, w3)

    act2 = move(act, (0, 2), (1, 3))
    far_lo, _ = lax.optimization_barrier((far_lo, act))
    via_lo = move(far_lo, (0, 1))
    far_hi, _ = lax.optimization_barrier((far_hi, act))
    via_hi = move(far_hi, (0, 1))
    act_late, via_lo, via_hi = lax.optimization_barrier((act, via_lo, via_hi))
    act1 = move(act_late, (0, 1), (1, 2), (2, 3))

    first = pl.BlockSpec((block, channels), lambda step: (jnp.minimum(step, BLOCKS - 1), 0))
    second = pl.BlockSpec((block, channels), lambda step: (jnp.maximum(step - BLOCKS, 0), 0))
    both = pl.BlockSpec((block, channels), lambda step: (step % BLOCKS, 0))
    lo = pl.BlockSpec((block, channels), lambda step: (jnp.minimum(step, BLOCKS // 2 - 1), 0))
    hi = pl.BlockSpec(
        (block, channels),
        lambda step: (jnp.clip(step - BLOCKS // 2, 0, BLOCKS // 2 - 1), 0),
    )
    grads_shape = jax.ShapeDtypeStruct((12 * channels, channels), F32)
    grad_in, grads = pl.pallas_call(
        functools.partial(backward_kernel, width),
        grid=(2 * BLOCKS,),
        out_shape=(frame, grads_shape),
        in_specs=[second, both, first, lo, hi, lo, hi, first, first, whole(wt), whole(wf)],
        out_specs=(second, whole(grads_shape)),
        scratch_shapes=[
            padded,
            pltpu.VMEM((3, channels, channels), F32),
            pltpu.VMEM((3, channels, 3 * channels), F32),
        ],
        compiler_params=params,
        cost_estimate=pl.CostEstimate(
            flops=48 * cells * channels * channels,
            bytes_accessed=18 * cells * channels,
            transcendentals=0,
        ),
        name="backward",
    )(x, cot, near, far_lo, far_hi, via_lo, via_hi, act, slope, wt, wf)

    reduced = reduce_all(grads)

    block_out = pl.pallas_call(
        temporal_kernel,
        grid=(BLOCKS,),
        out_shape=frame,
        in_specs=[rows_spec] * 4 + [whole(temporal_weight)],
        out_specs=rows_spec,
        compiler_params=params,
        cost_estimate=pl.CostEstimate(
            flops=6 * cells * channels * channels,
            bytes_accessed=10 * cells * channels,
            transcendentals=0,
        ),
        name="temporal",
    )(x, act, act1, act2, temporal_weight)

    grad_scale = 1.0 / math.sqrt(slab_rows * sp_count * lax.axis_size("dp") * width)
    scaled = reduced.astype(F32) * grad_scale
    grad_spatial = scaled[: 9 * channels].reshape(3, 3, channels, channels)
    grad_temporal = scaled[9 * channels :].reshape(3, channels, channels)
    return (
        block_out.reshape(frames_in.shape),
        grad_in.reshape(frames_in.shape),
        grad_spatial,
        grad_temporal,
    )


def solution(mesh):
    placed = (P(("dp", "sp"), None, None), P(), P(), P(("dp", "sp"), None, None))
    return jax.shard_map(
        local,
        mesh=mesh,
        in_specs=placed,
        out_specs=(P(("dp", "sp"), None, None), P(("dp", "sp"), None, None), P(), P()),
        check_vma=False,
    )
```

```python
import functools
import math

import jax
import jax.numpy as jnp
from jax import lax
from jax.experimental import pallas as pl
from jax.experimental.pallas import tpu as pltpu
from jax.sharding import PartitionSpec as P

FRAMES = 4
BLOCKS = 4
VMEM_LIMIT = 50 * 1024 * 1024
MESH = pl.DeviceIdType.MESH
F32 = jnp.float32
BF16 = jnp.bfloat16


def store_shifted(dest, offset, values, width):
    cells, channels = values.shape
    column = lax.broadcasted_iota(jnp.int32, (cells, channels), 0) % width
    before = jnp.where(column == 0, 0.0, pltpu.roll(values, 1, axis=0))
    after = jnp.where(column == width - 1, 0.0, pltpu.roll(values, cells - 1, axis=0))
    dest[pl.ds(offset, cells), 0:channels] = before.astype(BF16)
    dest[pl.ds(offset, cells), channels : 2 * channels] = values.astype(BF16)
    dest[pl.ds(offset, cells), 2 * channels : 3 * channels] = after.astype(BF16)


def zero_edges(dest, width):
    rows, lanes = dest.shape
    dest[0:width] = jnp.zeros((width, lanes), BF16)
    dest[rows - width : rows] = jnp.zeros((width, lanes), BF16)


def forward_kernel(width, x_ref, w_ref, act_ref, slope_ref, x3):
    step = pl.program_id(0)
    cells, channels = act_ref.shape

    @pl.when(step == 0)
    def _():
        zero_edges(x3, width)
        for block in range(BLOCKS):
            store_shifted(
                x3,
                width + block * cells,
                x_ref[block * cells : (block + 1) * cells].astype(F32),
                width,
            )

    base = pl.multiple_of(step * cells, cells)
    pre = jnp.zeros((cells, channels), F32)
    for tap in range(3):
        pre = pre + jnp.dot(
            x3[pl.ds(base + tap * width, cells), :], w_ref[tap], preferred_element_type=F32
        )
    sigma = jax.nn.sigmoid(pre)
    act_ref[...] = (pre * sigma).astype(BF16)
    slope_ref[...] = sigma * (1.0 + pre * (1.0 - sigma))


def backward_kernel(
    width, x_ref, cot_ref, cot1_ref, cot2_ref, act_ref, slope_ref, wt_ref, wf_ref,
    grad_in_ref, grads_ref, g3, temporal, spatial,
):
    step = pl.program_id(0)
    cells, channels = act_ref.shape

    @pl.when(step == 0)
    def _():
        zero_edges(g3, width)
        temporal[...] = jnp.zeros_like(temporal)
        spatial[...] = jnp.zeros_like(spatial)

    @pl.when(step < BLOCKS)
    def _():
        act_t = act_ref[...].T
        grad_act = jnp.zeros((cells, channels), F32)
        for tap, ref in enumerate((cot_ref, cot1_ref, cot2_ref)):
            grad_act = grad_act + jnp.dot(ref[...], wt_ref[tap], preferred_element_type=F32)
            temporal[tap] += jnp.dot(act_t, ref[...], preferred_element_type=F32)
        grad_pre = grad_act * slope_ref[...]
        store_shifted(g3, pl.multiple_of(width + step * cells, width), grad_pre, width)

    @pl.when(step >= BLOCKS)
    def _():
        base = pl.multiple_of((step - BLOCKS) * cells, cells)
        x_t = x_ref[...].T
        grad_in = cot_ref[...].astype(F32)
        for tap in range(3):
            window = g3[pl.ds(base + tap * width, cells), :]
            grad_in = grad_in + jnp.dot(window, wf_ref[tap], preferred_element_type=F32)
            spatial[tap] += jnp.dot(x_t, window, preferred_element_type=F32)
        grad_in_ref[...] = grad_in.astype(BF16)

    @pl.when(step == 2 * BLOCKS - 1)
    def _():
        for tap_row in range(3):
            for tap_col in range(3):
                place = (2 - tap_row) * 3 + 2 - tap_col
                grads_ref[place * channels : (place + 1) * channels] = spatial[
                    tap_row, :, tap_col * channels : (tap_col + 1) * channels
                ]
        for tap in range(3):
            grads_ref[(9 + tap) * channels : (10 + tap) * channels] = temporal[tap]


def temporal_kernel(x_ref, act_ref, act1_ref, act2_ref, w_ref, out_ref):
    total = jnp.dot(act_ref[...], w_ref[0], preferred_element_type=F32)
    total = total + jnp.dot(act1_ref[...], w_ref[1], preferred_element_type=F32)
    total = total + jnp.dot(act2_ref[...], w_ref[2], preferred_element_type=F32)
    total = total.astype(BF16).astype(F32)
    out_ref[...] = (x_ref[...].astype(F32) + total).astype(BF16)


def reduce_kernel(bits, chunks, grads_ref, full_ref, total, *scratch):
    levels = len(bits)
    staged = scratch[:chunks]
    recvs = scratch[chunks : chunks + chunks * levels]
    send_sem, recv_sem, back_send, back_recv = scratch[chunks + chunks * levels :]
    here = {name: lax.axis_index(name) for name in ("dp", "sp")}

    def partner(name, bit):
        mine = (here[name] // (1 << bit)) % 2
        ids = dict(here)
        ids[name] = here[name] + (1 - 2 * mine) * (1 << bit)
        return mine, (ids["dp"], ids["sp"])

    partners = [partner(name, bit) for name, bit in bits]
    barrier = pltpu.get_barrier_semaphore()
    for _, device in partners:
        pl.semaphore_signal(barrier, inc=1, device_id=device, device_id_type=MESH)
    pl.semaphore_wait(barrier, levels)

    rows = grads_ref.shape[0] // chunks
    half = grads_ref.shape[1] // 2
    rest = partners[1:]
    orders = []
    for chunk in range(chunks):
        turn = chunk % len(rest)
        orders.append(partners[:1] + rest[turn:] + rest[:turn])

    def send(chunk, level, source, dest, send_sems, recv_sems):
        copy = pltpu.make_async_remote_copy(
            src_ref=source,
            dst_ref=dest,
            send_sem=send_sems.at[chunk * levels + level],
            recv_sem=recv_sems.at[chunk * levels + level],
            device_id=orders[chunk][level][1],
            device_id_type=MESH,
        )
        copy.start()
        return copy

    mine = partners[0][0]
    keep = pl.multiple_of(mine * half, half)
    give = pl.multiple_of((1 - mine) * half, half)
    copies = [
        send(
            chunk, 0, grads_ref.at[chunk * rows : (chunk + 1) * rows, pl.ds(give, half)],
            recvs[chunk * levels], send_sem, recv_sem,
        )
        for chunk in range(chunks)
    ]
    for chunk in range(chunks):
        copies[chunk].wait()
        place = pl.ds(chunk * rows, rows)
        total[place, :] = grads_ref[place, pl.ds(keep, half)] + recvs[chunk * levels][...]
    starts = [[chunk * rows] for chunk in range(chunks)]
    size = rows
    for level in range(1, levels):
        size = size // 2
        copies = []
        for chunk in range(chunks):
            mine = orders[chunk][level][0]
            start = starts[chunk][-1]
            own = pl.multiple_of(start + mine * size, 16)
            other = pl.multiple_of(start + (1 - mine) * size, 16)
            source = total.at[pl.ds(other, size), :]
            if level == 1:
                staged[chunk][...] = total[pl.ds(other, size), :].astype(BF16)
                source = staged[chunk]
            dest = recvs[chunk * levels + level]
            copies.append(send(chunk, level, source, dest, send_sem, recv_sem))
            starts[chunk].append(own)
        for chunk in range(chunks):
            copies[chunk].wait()
            arrived = recvs[chunk * levels + level][...].astype(F32)
            total[pl.ds(starts[chunk][-1], size), :] += arrived
    for chunk in range(chunks):
        place = pl.ds(starts[chunk][-1], size)
        full_ref[place, pl.ds(keep, half)] = total[place, :].astype(BF16)
    for level in range(levels - 1, -1, -1):
        copies = []
        for chunk in range(chunks):
            place = full_ref.at[pl.ds(starts[chunk][level], size), pl.ds(keep, half)]
            copies.append(send(chunk, level, place, place, back_send, back_recv))
        for copy in copies:
            copy.wait()
        size = size * 2


def reduce_all(grads):
    bits = []
    for name in ("dp", "sp"):
        count = lax.axis_size(name)
        bits += [(name, bit) for bit in range(count.bit_length() - 1)]
    total_rows, channels = grads.shape
    half = channels // 2
    chunks = 3
    rows = total_rows // chunks
    levels = len(bits)
    staged = [pltpu.VMEM((rows // 2, half), BF16)] * chunks
    recvs = [
        pltpu.VMEM((rows >> level, half), BF16 if level == 1 else F32)
        for _ in range(chunks)
        for level in range(levels)
    ]
    semaphores = [pltpu.SemaphoreType.DMA((chunks * levels,))] * 4
    return pl.pallas_call(
        functools.partial(reduce_kernel, bits, chunks),
        out_shape=jax.ShapeDtypeStruct(grads.shape, BF16),
        in_specs=[pl.BlockSpec(memory_space=pltpu.VMEM)],
        out_specs=pl.BlockSpec(memory_space=pltpu.VMEM),
        scratch_shapes=[pltpu.VMEM((total_rows, half), F32)] + staged + recvs + semaphores,
        compiler_params=pltpu.CompilerParams(
            collective_id=0, has_side_effects=True, vmem_limit_bytes=VMEM_LIMIT
        ),
        name="reduce_all",
    )(grads)


def whole(array):
    return pl.BlockSpec(array.shape, lambda step: (0,) * array.ndim)


def local(frames_in, spatial_weight, temporal_weight, cotangent):
    slab_rows, width, channels = frames_in.shape
    sp_count = lax.axis_size("sp")
    cells = slab_rows * width
    block = cells // BLOCKS
    x = frames_in.reshape(cells, channels)
    cot = cotangent.reshape(cells, channels)
    params = pltpu.CompilerParams(
        dimension_semantics=("arbitrary",), vmem_limit_bytes=VMEM_LIMIT
    )

    def shift(values, by):
        pairs = [
            (i, i + by)
            for i in range(sp_count)
            if 0 <= i + by < sp_count and (i + by) // FRAMES == i // FRAMES
        ]
        return lax.ppermute(values, "sp", pairs)

    cot1 = shift(cot, -1)
    cot2 = shift(cot, -2)

    w3 = spatial_weight.reshape(3, 3 * channels, channels)
    wf = spatial_weight[::-1, ::-1].transpose(0, 1, 3, 2).reshape(3, 3 * channels, channels)
    wt = temporal_weight.transpose(0, 2, 1)
    rows_spec = pl.BlockSpec((block, channels), lambda step: (step, 0))
    frame = jax.ShapeDtypeStruct((cells, channels), BF16)
    padded = pltpu.VMEM((cells + 2 * width, 3 * channels), BF16)

    act, slope = pl.pallas_call(
        functools.partial(forward_kernel, width),
        grid=(BLOCKS,),
        out_shape=(frame, jax.ShapeDtypeStruct((cells, channels), F32)),
        in_specs=[whole(x), whole(w3)],
        out_specs=(rows_spec, rows_spec),
        scratch_shapes=[padded],
        compiler_params=params,
        cost_estimate=pl.CostEstimate(
            flops=18 * cells * channels * channels,
            bytes_accessed=8 * cells * channels,
            transcendentals=2 * cells * channels,
        ),
        name="forward",
    )(x, w3)

    act1 = shift(act, 1)
    act2 = shift(act, 2)

    first = pl.BlockSpec((block, channels), lambda step: (jnp.minimum(step, BLOCKS - 1), 0))
    second = pl.BlockSpec((block, channels), lambda step: (jnp.maximum(step - BLOCKS, 0), 0))
    both = pl.BlockSpec((block, channels), lambda step: (step % BLOCKS, 0))
    grads_shape = jax.ShapeDtypeStruct((12 * channels, channels), F32)
    grad_in, grads = pl.pallas_call(
        functools.partial(backward_kernel, width),
        grid=(2 * BLOCKS,),
        out_shape=(frame, grads_shape),
        in_specs=[second, both, first, first, first, first, whole(wt), whole(wf)],
        out_specs=(second, whole(grads_shape)),
        scratch_shapes=[
            padded,
            pltpu.VMEM((3, channels, channels), F32),
            pltpu.VMEM((3, channels, 3 * channels), F32),
        ],
        compiler_params=params,
        cost_estimate=pl.CostEstimate(
            flops=48 * cells * channels * channels,
            bytes_accessed=18 * cells * channels,
            transcendentals=0,
        ),
        name="backward",
    )(x, cot, cot1, cot2, act, slope, wt, wf)

    reduced = reduce_all(grads)

    block_out = pl.pallas_call(
        temporal_kernel,
        grid=(BLOCKS,),
        out_shape=frame,
        in_specs=[rows_spec] * 4 + [whole(temporal_weight)],
        out_specs=rows_spec,
        compiler_params=params,
        cost_estimate=pl.CostEstimate(
            flops=6 * cells * channels * channels,
            bytes_accessed=10 * cells * channels,
            transcendentals=0,
        ),
        name="temporal",
    )(x, act, act1, act2, temporal_weight)

    grad_scale = 1.0 / math.sqrt(slab_rows * sp_count * lax.axis_size("dp") * width)
    scaled = reduced.astype(F32) * grad_scale
    grad_spatial = scaled[: 9 * channels].reshape(3, 3, channels, channels)
    grad_temporal = scaled[9 * channels :].reshape(3, channels, channels)
    return (
        block_out.reshape(frames_in.shape),
        grad_in.reshape(frames_in.shape),
        grad_spatial,
        grad_temporal,
    )


def solution(mesh):
    placed = (P(("dp", "sp"), None, None), P(), P(), P(("dp", "sp"), None, None))
    return jax.shard_map(
        local,
        mesh=mesh,
        in_specs=placed,
        out_specs=(P(("dp", "sp"), None, None), P(("dp", "sp"), None, None), P(), P()),
        check_vma=False,
    )
```

```python
import functools
import math

import jax
import jax.numpy as jnp
from jax import lax
from jax.experimental import pallas as pl
from jax.experimental.pallas import tpu as pltpu
from jax.sharding import PartitionSpec as P

FRAMES = 4
BLOCKS = 4
VMEM_LIMIT = 50 * 1024 * 1024
MESH = pl.DeviceIdType.MESH
F32 = jnp.float32
BF16 = jnp.bfloat16


def store_shifted(dest, offset, values, width):
    cells, channels = values.shape
    column = lax.broadcasted_iota(jnp.int32, (cells, channels), 0) % width
    before = jnp.where(column == 0, 0.0, pltpu.roll(values, 1, axis=0))
    after = jnp.where(column == width - 1, 0.0, pltpu.roll(values, cells - 1, axis=0))
    dest[pl.ds(offset, cells), 0:channels] = before.astype(BF16)
    dest[pl.ds(offset, cells), channels : 2 * channels] = values.astype(BF16)
    dest[pl.ds(offset, cells), 2 * channels : 3 * channels] = after.astype(BF16)


def zero_edges(dest, width):
    rows, lanes = dest.shape
    dest[0:width] = jnp.zeros((width, lanes), BF16)
    dest[rows - width : rows] = jnp.zeros((width, lanes), BF16)


def forward_kernel(width, x_ref, w_ref, act_ref, slope_ref, x3):
    step = pl.program_id(0)
    cells, channels = act_ref.shape

    @pl.when(step == 0)
    def _():
        zero_edges(x3, width)
        for block in range(BLOCKS):
            store_shifted(
                x3,
                width + block * cells,
                x_ref[block * cells : (block + 1) * cells].astype(F32),
                width,
            )

    base = pl.multiple_of(step * cells, cells)
    pre = jnp.zeros((cells, channels), F32)
    for tap in range(3):
        pre = pre + jnp.dot(
            x3[pl.ds(base + tap * width, cells), :], w_ref[tap], preferred_element_type=F32
        )
    sigma = jax.nn.sigmoid(pre)
    act_ref[...] = (pre * sigma).astype(BF16)
    slope_ref[...] = sigma * (1.0 + pre * (1.0 - sigma))


def backward_kernel(
    width, x_ref, cot_ref, near_ref, far_lo_ref, far_hi_ref, via_lo_ref, via_hi_ref, act_ref, slope_ref, wt_ref, wf_ref,
    grad_in_ref, grads_ref, g3, temporal, spatial,
):
    step = pl.program_id(0)
    cells, channels = act_ref.shape

    @pl.when(step == 0)
    def _():
        zero_edges(g3, width)
        temporal[...] = jnp.zeros_like(temporal)
        spatial[...] = jnp.zeros_like(spatial)

    @pl.when(step < BLOCKS)
    def _():
        act_t = act_ref[...].T
        grad_act = jnp.zeros((cells, channels), F32)
        low = step < BLOCKS // 2
        next1 = near_ref[...] + jnp.where(low, via_lo_ref[...], via_hi_ref[...])
        next2 = jnp.where(low, far_lo_ref[...], far_hi_ref[...])
        for tap, later in enumerate((cot_ref[...], next1, next2)):
            grad_act = grad_act + jnp.dot(later, wt_ref[tap], preferred_element_type=F32)
            temporal[tap] += jnp.dot(act_t, later, preferred_element_type=F32)
        grad_pre = grad_act * slope_ref[...]
        store_shifted(g3, pl.multiple_of(width + step * cells, width), grad_pre, width)

    @pl.when(step >= BLOCKS)
    def _():
        base = pl.multiple_of((step - BLOCKS) * cells, cells)
        x_t = x_ref[...].T
        grad_in = cot_ref[...].astype(F32)
        for tap in range(3):
            window = g3[pl.ds(base + tap * width, cells), :]
            grad_in = grad_in + jnp.dot(window, wf_ref[tap], preferred_element_type=F32)
            spatial[tap] += jnp.dot(x_t, window, preferred_element_type=F32)
        grad_in_ref[...] = grad_in.astype(BF16)

    @pl.when(step == 2 * BLOCKS - 1)
    def _():
        for tap_row in range(3):
            for tap_col in range(3):
                place = (2 - tap_row) * 3 + 2 - tap_col
                grads_ref[place * channels : (place + 1) * channels] = spatial[
                    tap_row, :, tap_col * channels : (tap_col + 1) * channels
                ]
        for tap in range(3):
            grads_ref[(9 + tap) * channels : (10 + tap) * channels] = temporal[tap]


def temporal_kernel(x_ref, act_ref, act1_ref, act2_ref, w_ref, out_ref):
    total = jnp.dot(act_ref[...], w_ref[0], preferred_element_type=F32)
    total = total + jnp.dot(act1_ref[...], w_ref[1], preferred_element_type=F32)
    total = total + jnp.dot(act2_ref[...], w_ref[2], preferred_element_type=F32)
    total = total.astype(BF16).astype(F32)
    out_ref[...] = (x_ref[...].astype(F32) + total).astype(BF16)


def reduce_kernel(bits, chunks, grads_ref, full_ref, total, *scratch):
    levels = len(bits)
    staged = scratch[:chunks]
    recvs = scratch[chunks : chunks + chunks * levels]
    send_sem, recv_sem, back_send, back_recv = scratch[chunks + chunks * levels :]
    here = {name: lax.axis_index(name) for name in ("dp", "sp")}

    def partner(name, bit):
        mine = (here[name] // (1 << bit)) % 2
        ids = dict(here)
        ids[name] = here[name] + (1 - 2 * mine) * (1 << bit)
        return mine, (ids["dp"], ids["sp"])

    partners = [partner(name, bit) for name, bit in bits]
    barrier = pltpu.get_barrier_semaphore()
    for _, device in partners:
        pl.semaphore_signal(barrier, inc=1, device_id=device, device_id_type=MESH)
    pl.semaphore_wait(barrier, levels)

    rows = grads_ref.shape[0] // chunks
    half = grads_ref.shape[1] // 2
    rest = partners[1:]
    orders = []
    for chunk in range(chunks):
        turn = chunk % len(rest)
        orders.append(partners[:1] + rest[turn:] + rest[:turn])

    def send(chunk, level, source, dest, send_sems, recv_sems):
        copy = pltpu.make_async_remote_copy(
            src_ref=source,
            dst_ref=dest,
            send_sem=send_sems.at[chunk * levels + level],
            recv_sem=recv_sems.at[chunk * levels + level],
            device_id=orders[chunk][level][1],
            device_id_type=MESH,
        )
        copy.start()
        return copy

    mine = partners[0][0]
    keep = pl.multiple_of(mine * half, half)
    give = pl.multiple_of((1 - mine) * half, half)
    copies = [
        send(
            chunk, 0, grads_ref.at[chunk * rows : (chunk + 1) * rows, pl.ds(give, half)],
            recvs[chunk * levels], send_sem, recv_sem,
        )
        for chunk in range(chunks)
    ]
    for chunk in range(chunks):
        copies[chunk].wait()
        place = pl.ds(chunk * rows, rows)
        total[place, :] = grads_ref[place, pl.ds(keep, half)] + recvs[chunk * levels][...]
    starts = [[chunk * rows] for chunk in range(chunks)]
    size = rows
    for level in range(1, levels):
        size = size // 2
        copies = []
        for chunk in range(chunks):
            mine = orders[chunk][level][0]
            start = starts[chunk][-1]
            own = pl.multiple_of(start + mine * size, 16)
            other = pl.multiple_of(start + (1 - mine) * size, 16)
            source = total.at[pl.ds(other, size), :]
            if level == 1:
                staged[chunk][...] = total[pl.ds(other, size), :].astype(BF16)
                source = staged[chunk]
            dest = recvs[chunk * levels + level]
            copies.append(send(chunk, level, source, dest, send_sem, recv_sem))
            starts[chunk].append(own)
        for chunk in range(chunks):
            copies[chunk].wait()
            arrived = recvs[chunk * levels + level][...].astype(F32)
            total[pl.ds(starts[chunk][-1], size), :] += arrived
    for chunk in range(chunks):
        place = pl.ds(starts[chunk][-1], size)
        full_ref[place, pl.ds(keep, half)] = total[place, :].astype(BF16)
    for level in range(levels - 1, -1, -1):
        copies = []
        for chunk in range(chunks):
            place = full_ref.at[pl.ds(starts[chunk][level], size), pl.ds(keep, half)]
            copies.append(send(chunk, level, place, place, back_send, back_recv))
        for copy in copies:
            copy.wait()
        size = size * 2


def reduce_all(grads):
    bits = []
    for name in ("dp", "sp"):
        count = lax.axis_size(name)
        bits += [(name, bit) for bit in range(count.bit_length() - 1)]
    total_rows, channels = grads.shape
    half = channels // 2
    chunks = 3
    rows = total_rows // chunks
    levels = len(bits)
    staged = [pltpu.VMEM((rows // 2, half), BF16)] * chunks
    recvs = [
        pltpu.VMEM((rows >> level, half), BF16 if level == 1 else F32)
        for _ in range(chunks)
        for level in range(levels)
    ]
    semaphores = [pltpu.SemaphoreType.DMA((chunks * levels,))] * 4
    return pl.pallas_call(
        functools.partial(reduce_kernel, bits, chunks),
        out_shape=jax.ShapeDtypeStruct(grads.shape, BF16),
        in_specs=[pl.BlockSpec(memory_space=pltpu.VMEM)],
        out_specs=pl.BlockSpec(memory_space=pltpu.VMEM),
        scratch_shapes=[pltpu.VMEM((total_rows, half), F32)] + staged + recvs + semaphores,
        compiler_params=pltpu.CompilerParams(
            collective_id=0, has_side_effects=True, vmem_limit_bytes=VMEM_LIMIT
        ),
        name="reduce_all",
    )(grads)


def whole(array):
    return pl.BlockSpec(array.shape, lambda step: (0,) * array.ndim)


def local(frames_in, spatial_weight, temporal_weight, cotangent):
    slab_rows, width, channels = frames_in.shape
    sp_count = lax.axis_size("sp")
    cells = slab_rows * width
    block = cells // BLOCKS
    x = frames_in.reshape(cells, channels)
    cot = cotangent.reshape(cells, channels)
    params = pltpu.CompilerParams(
        dimension_semantics=("arbitrary",), vmem_limit_bytes=VMEM_LIMIT
    )

    def move(values, *steps):
        pairs = [
            (clip + source, clip + target)
            for clip in range(0, sp_count, FRAMES)
            for source, target in steps
        ]
        return lax.ppermute(values, "sp", pairs)

    middle = cells // 2
    far_lo = move(cot[:middle], (2, 0), (3, 1))
    near = move(cot, (1, 0), (3, 2))

    w3 = spatial_weight.reshape(3, 3 * channels, channels)
    wf = spatial_weight[::-1, ::-1].transpose(0, 1, 3, 2).reshape(3, 3 * channels, channels)
    wt = temporal_weight.transpose(0, 2, 1)
    rows_spec = pl.BlockSpec((block, channels), lambda step: (step, 0))
    frame = jax.ShapeDtypeStruct((cells, channels), BF16)
    padded = pltpu.VMEM((cells + 2 * width, 3 * channels), BF16)

    act, slope = pl.pallas_call(
        functools.partial(forward_kernel, width),
        grid=(BLOCKS,),
        out_shape=(frame, jax.ShapeDtypeStruct((cells, channels), F32)),
        in_specs=[whole(x), whole(w3)],
        out_specs=(rows_spec, rows_spec),
        scratch_shapes=[padded],
        compiler_params=params,
        cost_estimate=pl.CostEstimate(
            flops=18 * cells * channels * channels,
            bytes_accessed=8 * cells * channels,
            transcendentals=2 * cells * channels,
        ),
        name="forward",
    )(x, w3)

    far_lo, act = lax.optimization_barrier((far_lo, act))
    via_lo = move(far_lo, (0, 1))
    far_hi = move(lax.optimization_barrier((cot[middle:], far_lo))[0], (2, 0), (3, 1))
    act2 = move(act, (0, 2), (1, 3))
    via_hi = move(far_hi, (0, 1))
    act_late, via_lo, via_hi = lax.optimization_barrier((act, via_lo, via_hi))
    act1 = move(act_late, (0, 1), (1, 2), (2, 3))

    first = pl.BlockSpec((block, channels), lambda step: (jnp.minimum(step, BLOCKS - 1), 0))
    second = pl.BlockSpec((block, channels), lambda step: (jnp.maximum(step - BLOCKS, 0), 0))
    both = pl.BlockSpec((block, channels), lambda step: (step % BLOCKS, 0))
    lo = pl.BlockSpec((block, channels), lambda step: (jnp.minimum(step, BLOCKS // 2 - 1), 0))
    hi = pl.BlockSpec(
        (block, channels),
        lambda step: (jnp.clip(step - BLOCKS // 2, 0, BLOCKS // 2 - 1), 0),
    )
    grads_shape = jax.ShapeDtypeStruct((12 * channels, channels), F32)
    grad_in, grads = pl.pallas_call(
        functools.partial(backward_kernel, width),
        grid=(2 * BLOCKS,),
        out_shape=(frame, grads_shape),
        in_specs=[second, both, first, lo, hi, lo, hi, first, first, whole(wt), whole(wf)],
        out_specs=(second, whole(grads_shape)),
        scratch_shapes=[
            padded,
            pltpu.VMEM((3, channels, channels), F32),
            pltpu.VMEM((3, channels, 3 * channels), F32),
        ],
        compiler_params=params,
        cost_estimate=pl.CostEstimate(
            flops=48 * cells * channels * channels,
            bytes_accessed=18 * cells * channels,
            transcendentals=0,
        ),
        name="backward",
    )(x, cot, near, far_lo, far_hi, via_lo, via_hi, act, slope, wt, wf)

    reduced = reduce_all(grads)

    block_out = pl.pallas_call(
        temporal_kernel,
        grid=(BLOCKS,),
        out_shape=frame,
        in_specs=[rows_spec] * 4 + [whole(temporal_weight)],
        out_specs=rows_spec,
        compiler_params=params,
        cost_estimate=pl.CostEstimate(
            flops=6 * cells * channels * channels,
            bytes_accessed=10 * cells * channels,
            transcendentals=0,
        ),
        name="temporal",
    )(x, act, act1, act2, temporal_weight)

    grad_scale = 1.0 / math.sqrt(slab_rows * sp_count * lax.axis_size("dp") * width)
    scaled = reduced.astype(F32) * grad_scale
    grad_spatial = scaled[: 9 * channels].reshape(3, 3, channels, channels)
    grad_temporal = scaled[9 * channels :].reshape(3, channels, channels)
    return (
        block_out.reshape(frames_in.shape),
        grad_in.reshape(frames_in.shape),
        grad_spatial,
        grad_temporal,
    )


def solution(mesh):
    placed = (P(("dp", "sp"), None, None), P(), P(), P(("dp", "sp"), None, None))
    return jax.shard_map(
        local,
        mesh=mesh,
        in_specs=placed,
        out_specs=(P(("dp", "sp"), None, None), P(("dp", "sp"), None, None), P(), P()),
        check_vma=False,
    )
```
